128 devices in a mesh: row: 8 (over y, z_lo), col: 16 (over z_hi, x, core).
Axes of the slice: x: 4, y: 4, z: 4 (z_hi: 2, z_lo: 2; z = z_hi * 2 + z_lo), core: 2. Of those that a mesh axis runs over, the one named last changes fastest.
Arguments:
- x_tiles: float32 [8, 16, 12, 128, 128], P('row', 'col'), may hold values from -1.2 to 1.2
- x_where: int32 [8, 16, 12], P('row', 'col'), may hold values from 0 to 31, as said below
- keep_where: int32 [8, 16, 24], P('row', 'col'), may hold values from 0 to 31, as said below
Outputs:
- y_tiles: float32 [8, 16, 24, 128, 128], P('row', 'col')
The draws below stay inside these ranges and needn't reach their ends.
Inputs may be any that keep to these rules, and one draw needn't show every extreme that they name: `x_where`: on each device the 12 positions are distinct, each local row * 4 + local column of a block of 8 x 4 tiles. `keep_where`: on each device the 24 positions are distinct and ascending and include every position of x_where of the same device.
All inputs are finite; a program needn't handle non-finite values.
Results may differ from the reference program's by a relative error of at most 0.0003.
Values sent between devices are 32-bit elements; how exact they have to be, the bound alone decides.
No kernel may reach another device: no remote copies, remote signals or barrier semaphores. Data moves between devices by JAX's collectives and lax.ppermute only.
A program may use at most 128 MiB of HBM per device.

```python
import jax
import jax.numpy as jnp
from jax import lax

B = 128
TC = 4
SLOTS = 12
KEEP = 24
TR = 8
N_ROW = 8
N_COL = 16


def pattern_order(key):
    local = TR * TC
    scores = jax.random.randint(key, (N_ROW, N_COL, local), 0, 1 << 20)
    scores = scores * local + jnp.arange(local, dtype=jnp.int32)
    return jnp.argsort(scores, axis=-1, stable=True).astype(jnp.int32)


def draw_x_where(key, part):
    order = pattern_order(key)
    return order[:, :, :SLOTS]


def draw_keep_where(key, part):
    order = pattern_order(key)
    return jnp.sort(order[:, :, :KEEP], axis=-1).astype(jnp.int32)


def shard_levels(rng, dims, shards, smallest, high):
    loudness, own = 1.0, jax.random.fold_in(rng, 6)
    for position, parts in shards:
        draws = jnp.exp(jax.random.uniform(jax.random.fold_in(own, position), (parts,), jnp.float32, smallest / len(shards), high / len(shards)))
        loudness = loudness * jnp.repeat(draws, dims[position] // parts).reshape([-1 if axis == position else 1 for axis in range(len(dims))])
    return loudness


def bell_draw(stream_key, extent, scale, limit, shards=(), kind=jnp.bfloat16):
    values = scale * jax.random.normal(stream_key, extent, jnp.float32)
    if shards:
        values = values * shard_levels(stream_key, extent, shards, -0.22, 0.18)
    return jnp.clip(values, -limit, limit).astype(kind)


def setup_inputs(seed: int = 0) -> dict:
    streams_of = jax.random.split(jax.random.key(seed), 4)
    return {
        "x_tiles": bell_draw(streams_of[0], (N_ROW, N_COL, SLOTS, B, B), 0.2, 1.2, ((0, 8), (1, 16)), jnp.float32),
        "x_where": draw_x_where(jax.random.fold_in(streams_of[3], 71), 0),
        "keep_where": draw_keep_where(jax.random.fold_in(streams_of[3], 71), 0),
    }


def column_products(left_blocks, left_inner, right_padded, right_inner, right_column, tile_cols):
    matches = (left_inner[:, None, None] == right_inner[None, None, :]) & (right_column[None, None, :] == jnp.arange(tile_cols, dtype=jnp.int32)[None, :, None])
    numbers = jnp.arange(1, right_inner.shape[0] + 1, dtype=jnp.int32)
    chosen_slot = jnp.sum(jnp.where(matches, numbers[None, None, :], 0), axis=2).astype(jnp.int32)
    chosen = right_padded[chosen_slot]
    return jnp.einsum("nab,njbc->njac", left_blocks, chosen, precision=lax.Precision.HIGHEST)


def row_sum(products, left_rows, tile_rows):
    onehot = (left_rows[:, None] == jnp.arange(tile_rows, dtype=jnp.int32)[None, :]).astype(products.dtype)
    return jnp.einsum("nr,njac->rjac", onehot, products, precision=lax.Precision.HIGHEST)


def right_panel(blocks, places, tile_rows, tile_cols):
    groups = places.shape[0]
    places = places.reshape(groups, -1)
    right_inner = (jnp.arange(groups, dtype=jnp.int32)[:, None] * tile_rows + places // tile_cols).reshape(-1)
    right_column = (places % tile_cols).reshape(-1)
    flat = blocks.reshape((-1,) + blocks.shape[-2:])
    padded = jnp.concatenate([jnp.zeros((1,) + blocks.shape[-2:], blocks.dtype), flat], 0)
    return padded, right_inner, right_column


def place_tiles(blocks, places, kept_places):
    chooser = (kept_places[:, None] == places[None, :]).astype(blocks.dtype)
    return jnp.einsum("ks,sab->kab", chooser, blocks, precision=lax.Precision.HIGHEST)


def block_product(left_blocks, left_places, right_blocks, right_places):
    padded, right_inner, right_column = right_panel(right_blocks, right_places, TR, TC)
    owners_col = jnp.arange(N_COL, dtype=jnp.int32)[:, None]
    left_inner = (owners_col * TC + left_places % TC).reshape(-1)
    products = column_products(left_blocks.reshape((-1,) + left_blocks.shape[-2:]), left_inner, padded, right_inner, right_column, TC)
    return row_sum(products, (left_places // TC).reshape(-1), TR)


def reference(x_tiles, x_where, keep_where):
    indices = jnp.arange(N_ROW * N_COL, dtype=jnp.int32)

    def square_one(index):
        grid_row = index // N_COL
        grid_col = index % N_COL
        dense_block = block_product(x_tiles[grid_row], x_where[grid_row], x_tiles[:, grid_col], x_where[:, grid_col])
        return dense_block.reshape(TR * TC, B, B)[keep_where[grid_row, grid_col]]

    square = lax.map(square_one, indices).reshape(N_ROW, N_COL, KEEP, B, B)

    def sign_one(index):
        grid_row = index // N_COL
        grid_col = index % N_COL
        dense_block = block_product(x_tiles[grid_row], x_where[grid_row], square[:, grid_col], keep_where[:, grid_col])
        kept_places = keep_where[grid_row, grid_col]
        cubic = dense_block.reshape(TR * TC, B, B)[kept_places]
        linear = place_tiles(x_tiles[grid_row, grid_col], x_where[grid_row, grid_col], kept_places)
        return 1.5 * linear - 0.5 * cubic

    return lax.map(sign_one, indices).reshape(N_ROW, N_COL, KEEP, B, B)
```

```python
import functools

import jax
import jax.numpy as jnp
from jax import lax
from jax.experimental import pallas as pl
from jax.experimental.pallas import tpu as pltpu
from jax.sharding import PartitionSpec as P

B = 128
TC = 4
TR = 8
SLOTS = 12
KEEP = 24
N_ROW = 8
N_COL = 16
BODY = SLOTS * B
FIRST = 14
SECOND = KEEP - FIRST
LIMIT = 60 << 20

ANY = pl.BlockSpec(memory_space=pl.ANY)
VMEM = pl.BlockSpec(memory_space=pltpu.VMEM)
SMEM = pl.BlockSpec(memory_space=pltpu.SMEM)
F32 = jnp.float32
BF16 = jnp.bfloat16


def decode(i):
    r, c = divmod(i, N_COL)
    return r // 2, (c // 8) * 2 + r % 2, (c % 8) // 2, c % 2


def encode(y, z, x, core):
    return ((y % 4) * 2 + z % 2) * N_COL + ((z // 2) * 4 + x % 4) * 2 + core


MOVES = {
    "y+": lambda y, z, x, k: (y + 1, z, x, k),
    "y-": lambda y, z, x, k: (y - 1, z, x, k),
    "x+": lambda y, z, x, k: (y, z, x + 1, k),
    "x-": lambda y, z, x, k: (y, z, x - 1, k),
    "zl": lambda y, z, x, k: (y, z ^ 1, x, k),
    "zh": lambda y, z, x, k: (y, z ^ 2, x, k),
    "core": lambda y, z, x, k: (y, z, x, 1 - k),
}


def send(a, move):
    pairs = [(i, encode(*MOVES[move](*decode(i)))) for i in range(N_ROW * N_COL)]
    return lax.ppermute(a, ("row", "col"), pairs)


def cost(chunks, moved):
    flops = chunks * 0.5 * 2 * (TR * B) * (TR * B) * (TC * B)
    return pl.CostEstimate(flops=int(flops), bytes_accessed=int(moved * 0.5 / 3), transcendentals=0)


def dot(a, b):
    return jnp.dot(a, b, preferred_element_type=F32)


def block_of(where):
    row = pl.multiple_of((where >> 2) * B, B)
    col = pl.multiple_of((where & 3) * B, B)
    return pl.ds(row, B), pl.ds(col, B)


def tile_of(t):
    return pl.ds(pl.multiple_of(t * B, B), B)


def split(v):
    hi = v.astype(BF16)
    return hi, (v - hi.astype(F32)).astype(BF16)


class Chunk:
    def __init__(self, refs):
        (self.raw, self.meta, self.braw, self.bmeta, self.ahi, self.alo, self.bhi, self.blo) = refs[:8]
        self.sem, self.bsem, self.asem = refs[8:]

    shapes = [
        pltpu.VMEM((2, 2, BODY, B), F32),
        pltpu.SMEM((2, 2, 8, B), F32),
        pltpu.VMEM((2, KEEP * B, B), F32),
        pltpu.SMEM((2, 8, B), F32),
        pltpu.VMEM((TR * B, TR * B), BF16),
        pltpu.VMEM((TR * B, TR * B), BF16),
        pltpu.VMEM((TR * B, TC * B), BF16),
        pltpu.VMEM((TR * B, TC * B), BF16),
        pltpu.SemaphoreType.DMA((2, 4)),
        pltpu.SemaphoreType.DMA((2, 4)),
        pltpu.SemaphoreType.DMA,
    ]

    def clear(self):
        for ref in (self.ahi, self.alo, self.bhi, self.blo):
            ref[...] = jnp.zeros(ref.shape, BF16)

    def fetch(self, slot, which, core, pairs):
        def start(ref, half):
            pltpu.make_async_copy(
                ref.at[pl.ds(0, BODY), :], self.raw.at[slot, half], self.sem.at[slot, half]
            ).start()
            pltpu.make_async_copy(
                ref.at[pl.ds(BODY, 8), :], self.meta.at[slot, half], self.sem.at[slot, 2 + half]
            ).start()

        for j, (own, other) in enumerate(pairs):

            @pl.when(which == j)
            def _():
                start(own, core)
                start(other, 1 - core)

    def arrive(self, slot, ref):
        for half in range(2):
            pltpu.make_async_copy(
                ref.at[pl.ds(0, BODY), :], self.raw.at[slot, half], self.sem.at[slot, half]
            ).wait()
            pltpu.make_async_copy(
                ref.at[pl.ds(BODY, 8), :], self.meta.at[slot, half], self.sem.at[slot, 2 + half]
            ).wait()

    def piece(self, slot, ref, start, at, rows, sem):
        return pltpu.make_async_copy(
            ref.at[pl.ds(start, rows), :], self.braw.at[slot, pl.ds(at, rows), :], self.bsem.at[slot, sem]
        )

    def note(self, slot, ref, start):
        return pltpu.make_async_copy(ref.at[pl.ds(start, 8), :], self.bmeta.at[slot], self.bsem.at[slot, 3])

    def load_a(self, slot):
        for half in range(2):

            @pl.loop(0, SLOTS, unroll=4)
            def _(t):
                where = self.meta[slot, half, 0, t].astype(jnp.int32)
                row = pl.ds(pl.multiple_of((where >> 2) * B, B), B)
                col = pl.ds(pl.multiple_of(((where & 3) + TC * half) * B, B), B)
                hi, lo = split(self.raw[slot, half, tile_of(t), :])
                self.ahi[row, col] = hi
                self.alo[row, col] = lo

    def wipe_a(self, slot):
        for half in range(2):

            @pl.loop(0, SLOTS, unroll=4)
            def _(t):
                where = self.meta[slot, half, 0, t].astype(jnp.int32)
                row = pl.ds(pl.multiple_of((where >> 2) * B, B), B)
                col = pl.ds(pl.multiple_of(((where & 3) + TC * half) * B, B), B)
                self.ahi[row, col] = jnp.zeros((B, B), BF16)
                self.alo[row, col] = jnp.zeros((B, B), BF16)

    def load_b(self, slot, n, lane):
        @pl.loop(0, n, unroll=4)
        def _(t):
            at = block_of(self.bmeta[slot, 0, lane + t].astype(jnp.int32))
            hi, lo = split(self.braw[slot, tile_of(t), :])
            self.bhi[at] = hi
            self.blo[at] = lo

    def wipe_b(self, slot, n, lane):
        @pl.loop(0, n, unroll=4)
        def _(t):
            at = block_of(self.bmeta[slot, 0, lane + t].astype(jnp.int32))
            self.bhi[at] = jnp.zeros((B, B), BF16)
            self.blo[at] = jnp.zeros((B, B), BF16)

    def multiply(self, acc):
        for jp in range(2):
            cols = slice(jp * 2 * B, (jp + 1) * 2 * B)
            bh, bl = self.bhi[:, cols], self.blo[:, cols]
            acc[:, cols] = acc[:, cols] + (
                dot(self.ahi[...], bh) + dot(self.alo[...], bh) + dot(self.ahi[...], bl)
            )


def pack(acc, keep, start, n, out, scale=None):
    @pl.loop(0, n, unroll=4)
    def _(t):
        v = acc[block_of(keep[start + t])]
        out[tile_of(t), :] = v if scale is None else scale * v


def square_kernel(n_pair, cuts, first, last, *refs):
    refs = list(refs)
    ids = refs.pop(0)
    pairs = [(refs.pop(0), refs.pop(0)) for _ in range(n_pair)]
    bs = [[refs.pop(0) for _ in range(n)] for n in cuts]
    acc_in = None if first else refs.pop(0)
    if last:
        keep, out1, out2, acc = refs.pop(0), refs.pop(0), refs.pop(0), refs.pop(0)
    else:
        acc = refs.pop(0)
    chunk = Chunk(refs)
    count, core = ids[0], ids[1]

    def fetch(t):
        slot = lax.rem(t, 2)
        chunk.fetch(slot, ids[2 + 2 * t], core, pairs)
        for j, parts in enumerate(bs):

            @pl.when(ids[3 + 2 * t] == j)
            def _():
                half = BODY // 2
                if len(parts) == 1:
                    chunk.piece(slot, parts[0], 0, 0, half, 0).start()
                    chunk.piece(slot, parts[0], half, half, half, 1).start()
                    chunk.note(slot, parts[0], BODY).start()
                else:
                    chunk.piece(slot, parts[0], 0, 0, half, 0).start()
                    chunk.piece(slot, parts[1], 0, half, half, 1).start()
                    chunk.note(slot, parts[1], half).start()

    if not first:
        pltpu.make_async_copy(acc_in, acc, chunk.asem).start()

    @pl.when(count > 0)
    def _():
        fetch(jnp.int32(0))

    chunk.clear()
    if first:
        acc[...] = jnp.zeros(acc.shape, F32)
    else:
        pltpu.make_async_copy(acc_in, acc, chunk.asem).wait()

    @pl.loop(0, count)
    def _(t):
        slot = lax.rem(t, 2)

        @pl.when(t + 1 < count)
        def _():
            fetch(t + 1)

        chunk.arrive(slot, pairs[0][0])
        for part in range(2):
            chunk.piece(slot, bs[0][0], 0, part * (BODY // 2), BODY // 2, part).wait()
        chunk.note(slot, bs[0][0], 0).wait()
        chunk.load_a(slot)
        chunk.load_b(slot, SLOTS, 0)
        chunk.multiply(acc)

        @pl.when(t + 1 < count)
        def _():
            chunk.wipe_a(slot)
            chunk.wipe_b(slot, SLOTS, 0)

    if last:
        pack(acc, keep, 0, SECOND, out2)
        pack(acc, keep, SECOND, FIRST, out1)


ACC = jax.ShapeDtypeStruct((TR * B, TC * B), F32)


def square_part(ids, pairs, bs, acc, keep=None, chunks=3):
    last = keep is not None
    args = [ids] + [p for pair in pairs for p in pair] + [p for parts in bs for p in parts]
    specs = [SMEM] + [ANY] * (len(args) - 1)
    if acc is not None:
        args.append(acc)
        specs.append(ANY)
    if last:
        args.append(keep)
        specs.append(SMEM)
    packed = (
        jax.ShapeDtypeStruct((FIRST * B, B), F32),
        jax.ShapeDtypeStruct((SECOND * B, B), F32),
    )
    return pl.pallas_call(
        functools.partial(square_kernel, len(pairs), [len(p) for p in bs], acc is None, last),
        out_shape=packed if last else ACC,
        in_specs=specs,
        out_specs=(VMEM, VMEM) if last else VMEM,
        scratch_shapes=([pltpu.VMEM(ACC.shape, F32)] if last else []) + Chunk.shapes,
        compiler_params=pltpu.CompilerParams(vmem_limit_bytes=LIMIT),
        cost_estimate=cost(chunks, chunks * 4 << 20),
        name="square_part",
    )(*args)


def cubic_kernel(slots, groups, n_pair, head, last, *refs):
    refs = list(refs)
    ids = refs.pop(0)
    pairs = [(refs.pop(0), refs.pop(0)) for _ in range(n_pair)]
    notes = [refs.pop(0) for _ in slots]
    pieces = [[refs.pop(0) for _ in group] for group in groups]
    start = refs.pop(0)
    where_x = refs.pop(0) if head else None
    if last:
        keep, out, acc = refs.pop(0), refs.pop(0), refs.pop(0)
    else:
        acc = refs.pop(0)
    chunk = Chunk(refs)
    core = ids[0]

    def fetch(s):
        chunk.fetch(s % 2, ids[1 + slots[s]], core, pairs)
        copies = [
            chunk.piece(s % 2, ref, 0, at * B, n * B, j)
            for j, (ref, (at, n)) in enumerate(zip(pieces[s], groups[s]))
        ]
        copies.append(chunk.note(s % 2, notes[s], notes[s].shape[0] - 8))
        for cp in copies:
            cp.start()
        return copies

    if not head:
        pltpu.make_async_copy(start, acc, chunk.asem).start()
    loads = fetch(0)
    chunk.clear()
    if head:
        acc[...] = jnp.zeros(acc.shape, F32)

        @pl.loop(0, SLOTS)
        def _(t):
            acc[block_of(where_x[t])] = -3.0 * start[tile_of(t), :]

    else:
        pltpu.make_async_copy(start, acc, chunk.asem).wait()
    for s in range(len(slots)):
        following = fetch(s + 1) if s + 1 < len(slots) else None
        for cp in loads:
            cp.wait()
        loads = following
        chunk.load_b(s % 2, KEEP, SLOTS)
        chunk.arrive(s % 2, pairs[0][0])
        chunk.load_a(s % 2)
        chunk.multiply(acc)
        if s + 1 < len(slots):
            chunk.wipe_a(s % 2)
            chunk.wipe_b(s % 2, KEEP, SLOTS)
    if last:
        pack(acc, keep, 0, KEEP, out, -0.5)


def cubic_part(ids, slots, pairs, notes, blocks, start, x_where=None, keep=None):
    head, last = x_where is not None, keep is not None
    groups = [[(at, n) for _, at, n in group] for group in blocks]
    args = [ids] + [p for pair in pairs for p in pair] + list(notes)
    args += [ref for group in blocks for ref, _, _ in group]
    specs = [SMEM] + [ANY] * (len(args) - 1)
    args.append(start)
    specs.append(VMEM if head else ANY)
    for extra in (x_where, keep):
        if extra is not None:
            args.append(extra)
            specs.append(SMEM)
    n = len(blocks)
    return pl.pallas_call(
        functools.partial(cubic_kernel, slots, groups, len(pairs), head, last),
        out_shape=jax.ShapeDtypeStruct((KEEP * B, B), F32) if last else ACC,
        in_specs=specs,
        out_specs=VMEM,
        scratch_shapes=([pltpu.VMEM(ACC.shape, F32)] if last else []) + Chunk.shapes,
        compiler_params=pltpu.CompilerParams(vmem_limit_bytes=LIMIT),
        cost_estimate=cost(n, n * 4 << 20),
        name="cubic_part",
    )(*args)


def after(a, *others):
    return lax.optimization_barrier((a,) + others)[0]


def on_device(x_tiles, x_where, keep_where):
    r, c = lax.axis_index("row"), lax.axis_index("col")
    y, lo = r // 2, r % 2
    hi, x, core = c // 8, (c % 8) // 2, c % 2
    keep = keep_where[0, 0]
    own_where = x_where[0, 0]
    tiles = x_tiles[0, 0].reshape(BODY, B)
    meta = jnp.concatenate([own_where, keep]).astype(F32)
    meta = jnp.pad(meta[None], ((0, 7), (0, B - SLOTS - KEEP)))
    own = jnp.concatenate([tiles, meta], 0)

    numbers = jnp.arange(N_ROW, dtype=jnp.int32)
    a_slot = jnp.array([0, 2, 6, 1, 3, 5, 7, 4], jnp.int32)[(numbers - x) % 4 + 4 * (numbers // 4 != hi)]
    b_slot = jnp.array([0, 2, 3, 1, 4, 6, 7, 5], jnp.int32)[(numbers // 2 - y) % 4 + 4 * (numbers % 2 != lo)]
    early = (a_slot < 4) & (b_slot < 5)
    then = (a_slot < 6) & (b_slot < 7) & ~early

    def listed(mask):
        mask = mask.astype(jnp.int32)
        hit = ((jnp.cumsum(mask) - 1)[None, :] == numbers[:, None]) & (mask[None, :] == 1)
        pick = jnp.stack([a_slot, b_slot], 1)
        lists = jnp.sum(jnp.where(hit[:, :, None], pick[None], 0), 1).reshape(-1)
        return jnp.concatenate([jnp.sum(mask)[None], core[None], lists]).astype(jnp.int32)

    by_b = jnp.sum(jnp.where(b_slot[None, :] == numbers[:, None], a_slot[None, :], 0), 1)
    ids = jnp.concatenate([core[None], by_b]).astype(jnp.int32)
    list1, list2, list3 = listed(early), listed(then), listed(~early & ~then)

    zh = send(own, "zh")
    xp, xm, yp, ym = send(own, "x+"), send(own, "x-"), send(own, "y+"), send(own, "y-")
    zh, xp, xm, yp, ym, own_z, ids, list1, list2, list3 = lax.optimization_barrier(
        (zh, xp, xm, yp, ym, own, ids, list1, list2, list3)
    )
    xhp, xhm = send(zh, "x+"), send(zh, "x-")
    zl = send(own_z, "zl")
    zh_c, xp_c, xm_c, own_c = send(zh, "core"), send(xp, "core"), send(xm, "core"), send(own_z, "core")
    y2 = send(yp, "y+")
    xhp, xhm, zl, y2, xp_t = lax.optimization_barrier((xhp, xhm, zl, y2, xp))
    yzp, yzm = send(zl, "y+"), send(zl, "y-")
    x2, xh2 = send(xp_t, "x+"), send(xhm, "x-")
    pairs = [(own_z, own_c), (xp, xp_c), (xm, xm_c), (zh, zh_c)]
    b_all = [[own], [yp], [ym], [y2], [zl]]
    acc = square_part(list1, pairs, b_all, None, chunks=2)
    yzp, yzm, x2, xh2, xhp, xhm, acc = lax.optimization_barrier((yzp, yzm, x2, xh2, xhp, xhm, acc))
    half = BODY // 2
    yz2 = [send(yzp[:half], "y+"), send(yzm[half:], "y-")]
    xhp_c, xhm_c = send(xhp, "core"), send(xhm, "core")
    x2_c, xh2_c = send(x2, "core"), send(after(xh2, xhp_c), "core")
    pairs += [(xhp, xhp_c), (xhm, xhm_c)]
    b_all += [[yzp], [yzm]]
    acc = square_part(list2, pairs, b_all, acc, chunks=2)
    pairs += [(x2, x2_c), (xh2, xh2_c)]
    b_all += [yz2]
    s1, s2 = square_part(list3, pairs, b_all, acc, keep=keep, chunks=2)

    notes = [own, yp, ym, y2, zl, yzp, yzm, yz2[1]]

    def add(slots, blocks, start, **kw):
        chunks = [[(one, SECOND, FIRST)] + two for one, two in blocks]
        return cubic_part(ids, slots, pairs, [notes[j] for j in slots], chunks, start, **kw)

    def whole(two):
        return [(two, 0, SECOND)]

    def halves(two, three):
        return [(two, 0, SECOND // 2), (three, SECOND // 2, SECOND // 2)]

    cut = SECOND // 2 * B
    yp_2, ym_2 = send(s2, "y+"), send(s2, "y-")
    z_1 = send(s1, "zl")
    yp_1, ym_1 = send(s1, "y+"), send(s1, "y-")
    acc = add([0], [(s1, whole(s2))], tiles, x_where=own_where)
    z_2 = send(after(s2, z_1, acc), "zl")
    yp_2, ym_2, yp_1, ym_1, z_1, z_2, acc = lax.optimization_barrier((yp_2, ym_2, yp_1, ym_1, z_1, z_2, acc))
    yzp_2 = send(yp_2, "zl")
    yzp_1, yzm_1 = send(z_1, "y+"), send(z_1, "y-")
    y2_2a, y2_2b = send(yp_2[:cut], "y+"), send(ym_2[cut:], "y-")
    acc = add([4, 1], [(z_1, whole(z_2)), (yp_1, whole(yp_2))], acc)
    yzm_2 = send(after(ym_2, yzp_2, acc), "zl")
    acc = add([2], [(ym_1, whole(ym_2))], acc)
    yzp_1, yzm_1, y2_2a, y2_2b, yp_1t, acc = lax.optimization_barrier((yzp_1, yzm_1, y2_2a, y2_2b, yp_1, acc))
    y2_1, yz2_1 = send(yp_1t, "y+"), send(yzm_1, "y-")
    yz2_2a, yz2_2b = send(after(y2_2a, yzm_2), "zl"), send(after(y2_2b, yzm_2), "zl")
    acc = add([5, 6], [(yzp_1, whole(yzp_2)), (yzm_1, whole(yzm_2))], acc)
    out = add(
        [3, 7], [(y2_1, halves(y2_2a, y2_2b)), (yz2_1, halves(yz2_2a, yz2_2b))], acc, keep=keep
    )
    return out.reshape(1, 1, KEEP, B, B)


def solution(mesh):
    placed = (P("row", "col", None, None, None), P("row", "col", None), P("row", "col", None))
    return jax.shard_map(
        on_device,
        mesh=mesh,
        in_specs=placed,
        out_specs=P("row", "col", None, None, None),
        check_vma=False,
    )
```

```python
import functools

import jax
import jax.numpy as jnp
from jax import lax
from jax.experimental import pallas as pl
from jax.experimental.pallas import tpu as pltpu
from jax.sharding import PartitionSpec as P

B = 128
TC = 4
TR = 8
SLOTS = 12
KEEP = 24
N_ROW = 8
N_COL = 16
BODY = SLOTS * B
FIRST = 16
SECOND = KEEP - FIRST
LIMIT = 60 << 20

ANY = pl.BlockSpec(memory_space=pl.ANY)
VMEM = pl.BlockSpec(memory_space=pltpu.VMEM)
SMEM = pl.BlockSpec(memory_space=pltpu.SMEM)
F32 = jnp.float32
F8 = jnp.float8_e4m3fn
TOP = 240.0
REST = 256.0
CUBIC_COST = 1.0
BF16 = jnp.bfloat16


def decode(i):
    r, c = divmod(i, N_COL)
    return r // 2, (c // 8) * 2 + r % 2, (c % 8) // 2, c % 2


def encode(y, z, x, core):
    return ((y % 4) * 2 + z % 2) * N_COL + ((z // 2) * 4 + x % 4) * 2 + core


MOVES = {
    "y+": lambda y, z, x, k: (y + 1, z, x, k),
    "y-": lambda y, z, x, k: (y - 1, z, x, k),
    "x+": lambda y, z, x, k: (y, z, x + 1, k),
    "x-": lambda y, z, x, k: (y, z, x - 1, k),
    "zl": lambda y, z, x, k: (y, z ^ 1, x, k),
    "zh": lambda y, z, x, k: (y, z ^ 2, x, k),
    "core": lambda y, z, x, k: (y, z, x, 1 - k),
}


def send(a, move):
    pairs = [(i, encode(*MOVES[move](*decode(i)))) for i in range(N_ROW * N_COL)]
    return lax.ppermute(a, ("row", "col"), pairs)


def cost(chunks, moved):
    flops = chunks * 0.5 * 2 * (TR * B) * (TR * B) * (TC * B)
    return pl.CostEstimate(flops=int(flops), bytes_accessed=int(moved * 0.5 / 3), transcendentals=0)


def dot(a, b):
    return jnp.dot(a, b, preferred_element_type=F32)


def block_of(where):
    row = pl.multiple_of((where >> 2) * B, B)
    col = pl.multiple_of((where & 3) * B, B)
    return pl.ds(row, B), pl.ds(col, B)


def tile_of(t):
    return pl.ds(pl.multiple_of(t * B, B), B)


def split(v, scale):
    hi = v.astype(BF16)
    wide = hi.astype(F32)
    return hi, (wide * scale).astype(F8), ((v - wide) * scale * REST).astype(F8)


class Chunk:
    def __init__(self, refs):
        self.raw, self.meta, self.braw, self.bmeta = refs[:4]
        self.a, self.b = refs[4:7], refs[7:10]
        self.sem, self.bsem, self.asem = refs[10:]

    shapes = [
        pltpu.VMEM((2, 2, BODY, B), F32),
        pltpu.SMEM((2, 2, 8, B), F32),
        pltpu.VMEM((2, KEEP * B, B), F32),
        pltpu.SMEM((2, 8, B), F32),
        pltpu.VMEM((TR * B, TR * B), BF16),
        pltpu.VMEM((TR * B, TR * B), F8),
        pltpu.VMEM((TR * B, TR * B), F8),
        pltpu.VMEM((TR * B, TC * B), BF16),
        pltpu.VMEM((TR * B, TC * B), F8),
        pltpu.VMEM((TR * B, TC * B), F8),
        pltpu.SemaphoreType.DMA((2, 4)),
        pltpu.SemaphoreType.DMA((2, 4)),
        pltpu.SemaphoreType.DMA,
    ]

    def clear(self):
        for ref in self.a + self.b:
            ref[...] = jnp.zeros(ref.shape, ref.dtype)

    def fetch(self, slot, which, core, pairs):
        def start(ref, half):
            pltpu.make_async_copy(
                ref.at[pl.ds(0, BODY), :], self.raw.at[slot, half], self.sem.at[slot, half]
            ).start()
            pltpu.make_async_copy(
                ref.at[pl.ds(BODY, 8), :], self.meta.at[slot, half], self.sem.at[slot, 2 + half]
            ).start()

        for j, (own, other) in enumerate(pairs):

            @pl.when(which == j)
            def _():
                start(own, core)
                start(other, 1 - core)

    def arrive(self, slot, ref):
        for half in range(2):
            pltpu.make_async_copy(
                ref.at[pl.ds(0, BODY), :], self.raw.at[slot, half], self.sem.at[slot, half]
            ).wait()
            pltpu.make_async_copy(
                ref.at[pl.ds(BODY, 8), :], self.meta.at[slot, half], self.sem.at[slot, 2 + half]
            ).wait()

    def piece(self, slot, ref, start, at, rows, sem):
        return pltpu.make_async_copy(
            ref.at[pl.ds(start, rows), :], self.braw.at[slot, pl.ds(at, rows), :], self.bsem.at[slot, sem]
        )

    def note(self, slot, ref, start):
        return pltpu.make_async_copy(ref.at[pl.ds(start, 8), :], self.bmeta.at[slot], self.bsem.at[slot, 3])

    def each_a(self, slot, put):
        for half in range(2):

            @pl.loop(0, SLOTS, unroll=4)
            def _(t):
                where = self.meta[slot, half, 0, t].astype(jnp.int32)
                row = pl.ds(pl.multiple_of((where >> 2) * B, B), B)
                col = pl.ds(pl.multiple_of(((where & 3) + TC * half) * B, B), B)
                put((row, col), half, t)

    def load_a(self, slot):
        scale = jnp.minimum(self.meta[slot, 0, 1, 0], self.meta[slot, 1, 1, 0])

        def put(at, half, t):
            for ref, v in zip(self.a, split(self.raw[slot, half, tile_of(t), :], scale)):
                ref[at] = v

        self.each_a(slot, put)
        return jnp.maximum(self.meta[slot, 0, 1, 1], self.meta[slot, 1, 1, 1])

    def wipe_a(self, slot):
        def put(at, half, t):
            for ref in self.a:
                ref[at] = jnp.zeros((B, B), ref.dtype)

        self.each_a(slot, put)

    def load_b(self, slot, n, lane, measured):
        if measured:
            top = jnp.full((8, B), 1e-30, F32)
            for t in range(n):
                v = jnp.abs(self.braw[slot, t * B : (t + 1) * B, :])
                top = jnp.maximum(top, jnp.max(v.reshape(B // 8, 8, B), 0))
            top = jnp.max(top, (0, 1), keepdims=True)
            scale, back = TOP / top, top / TOP
        else:
            scale, back = self.bmeta[slot, 1, 0], self.bmeta[slot, 1, 1]

        @pl.loop(0, n, unroll=4)
        def _(t):
            at = block_of(self.bmeta[slot, 0, lane + t].astype(jnp.int32))
            for ref, v in zip(self.b, split(self.braw[slot, tile_of(t), :], scale)):
                ref[at] = v

        return back

    def wipe_b(self, slot, n, lane):
        @pl.loop(0, n, unroll=4)
        def _(t):
            at = block_of(self.bmeta[slot, 0, lane + t].astype(jnp.int32))
            for ref in self.b:
                ref[at] = jnp.zeros((B, B), ref.dtype)

    def multiply(self, acc, back):
        ah, ah8, al8 = self.a
        for jp in range(2):
            cols = slice(jp * 2 * B, (jp + 1) * 2 * B)
            bh, bh8, bl8 = (ref[:, cols] for ref in self.b)
            small = dot(al8[...], bh8) + dot(ah8[...], bl8)
            acc[:, cols] = acc[:, cols] + (dot(ah[...], bh) + small * back)


def pack(acc, keep, start, n, out, scale=None):
    @pl.loop(0, n, unroll=4)
    def _(t):
        v = acc[block_of(keep[start + t])]
        out[tile_of(t), :] = v if scale is None else scale * v


def square_kernel(n_pair, n_b, first, last, *refs):
    refs = list(refs)
    ids = refs.pop(0)
    pairs = [(refs.pop(0), refs.pop(0)) for _ in range(n_pair)]
    bs = [refs.pop(0) for _ in range(n_b)]
    acc_in = None if first else refs.pop(0)
    if last:
        keep, out, out1, out2, acc = (refs.pop(0) for _ in range(5))
    else:
        acc = refs.pop(0)
    chunk = Chunk(refs)
    count, core = ids[0], ids[1]

    def fetch(t):
        slot = lax.rem(t, 2)
        chunk.fetch(slot, ids[2 + 2 * t], core, pairs)
        for j, ref in enumerate(bs):

            @pl.when(ids[3 + 2 * t] == j)
            def _():
                chunk.piece(slot, ref, 0, 0, BODY, 0).start()
                chunk.note(slot, ref, BODY).start()

    @pl.when(count > 0)
    def _():
        fetch(jnp.int32(0))

    if not first:
        pltpu.make_async_copy(acc_in, acc, chunk.asem).start()
    chunk.clear()
    if first:
        acc[...] = jnp.zeros(acc.shape, F32)

    @pl.loop(0, count)
    def _(t):
        slot = lax.rem(t, 2)

        @pl.when(t + 1 < count)
        def _():
            fetch(t + 1)

        chunk.arrive(slot, pairs[0][0])
        chunk.piece(slot, bs[0], 0, 0, BODY, 0).wait()
        chunk.note(slot, bs[0], 0).wait()
        back = chunk.load_a(slot) * chunk.load_b(slot, SLOTS, 0, False) * (1.0 / REST)
        if not first:

            @pl.when(t == 0)
            def _():
                pltpu.make_async_copy(acc_in, acc, chunk.asem).wait()

        chunk.multiply(acc, back)

        @pl.when(t + 1 < count)
        def _():
            chunk.wipe_a(slot)
            chunk.wipe_b(slot, SLOTS, 0)

    if not first:

        @pl.when(count == 0)
        def _():
            pltpu.make_async_copy(acc_in, acc, chunk.asem).wait()

    if last:
        pack(acc, keep, 0, KEEP, out)
        pack(acc, keep, SECOND, FIRST, out1)
        pack(acc, keep, 0, SECOND, out2)


ACC = jax.ShapeDtypeStruct((TR * B, TC * B), F32)


def square_part(ids, pairs, bs, acc, keep=None, chunks=3):
    last = keep is not None
    args = [ids] + [p for pair in pairs for p in pair] + list(bs)
    specs = [SMEM] + [ANY] * (len(args) - 1)
    if acc is not None:
        args.append(acc)
        specs.append(ANY)
    if last:
        args.append(keep)
        specs.append(SMEM)
    packed = (
        jax.ShapeDtypeStruct((KEEP * B, B), F32),
        jax.ShapeDtypeStruct((FIRST * B, B), F32),
        jax.ShapeDtypeStruct((SECOND * B, B), F32),
    )
    return pl.pallas_call(
        functools.partial(square_kernel, len(pairs), len(bs), acc is None, last),
        out_shape=packed if last else ACC,
        in_specs=specs,
        out_specs=(VMEM,) * 3 if last else VMEM,
        scratch_shapes=([pltpu.VMEM(ACC.shape, F32)] if last else []) + Chunk.shapes,
        compiler_params=pltpu.CompilerParams(vmem_limit_bytes=LIMIT),
        cost_estimate=cost(chunks, chunks * 4 << 20),
        name="square_part",
    )(*args)


def cubic_kernel(slots, groups, n_pair, head, last, *refs):
    refs = list(refs)
    ids = refs.pop(0)
    pairs = [(refs.pop(0), refs.pop(0)) for _ in range(n_pair)]
    notes = [refs.pop(0) for _ in slots]
    pieces = [[refs.pop(0) for _ in group] for group in groups]
    start = refs.pop(0)
    where_x = refs.pop(0) if head else None
    if last:
        keep, out, acc = refs.pop(0), refs.pop(0), refs.pop(0)
    else:
        acc = refs.pop(0)
    chunk = Chunk(refs)
    core = ids[0]

    def fetch(s):
        chunk.fetch(s % 2, ids[1 + slots[s]], core, pairs)
        copies = [
            chunk.piece(s % 2, ref, 0, at * B, n * B, j)
            for j, (ref, (at, n)) in enumerate(zip(pieces[s], groups[s]))
        ]
        copies.append(chunk.note(s % 2, notes[s], notes[s].shape[0] - 8))
        for cp in copies:
            cp.start()
        return copies

    loads = fetch(0)
    if not head:
        pltpu.make_async_copy(start, acc, chunk.asem).start()
    chunk.clear()
    if head:
        acc[...] = jnp.zeros(acc.shape, F32)

        @pl.loop(0, SLOTS)
        def _(t):
            acc[block_of(where_x[t])] = -3.0 * start[tile_of(t), :]

    for s in range(len(slots)):
        following = fetch(s + 1) if s + 1 < len(slots) else None
        for cp in loads:
            cp.wait()
        loads = following
        back = chunk.load_b(s % 2, KEEP, SLOTS, True)
        chunk.arrive(s % 2, pairs[0][0])
        back = back * (chunk.load_a(s % 2) * (1.0 / REST))
        if s == 0 and not head:
            pltpu.make_async_copy(start, acc, chunk.asem).wait()
        chunk.multiply(acc, back)
        if s + 1 < len(slots):
            chunk.wipe_a(s % 2)
            chunk.wipe_b(s % 2, KEEP, SLOTS)
    if last:
        pack(acc, keep, 0, KEEP, out, -0.5)


def cubic_part(ids, slots, pairs, notes, blocks, start, x_where=None, keep=None):
    head, last = x_where is not None, keep is not None
    groups = [[(at, n) for _, at, n in group] for group in blocks]
    args = [ids] + [p for pair in pairs for p in pair] + list(notes)
    args += [ref for group in blocks for ref, _, _ in group]
    specs = [SMEM] + [ANY] * (len(args) - 1)
    args.append(start)
    specs.append(VMEM if head else ANY)
    for extra in (x_where, keep):
        if extra is not None:
            args.append(extra)
            specs.append(SMEM)
    n = len(blocks)
    return pl.pallas_call(
        functools.partial(cubic_kernel, slots, groups, len(pairs), head, last),
        out_shape=jax.ShapeDtypeStruct((KEEP * B, B), F32) if last else ACC,
        in_specs=specs,
        out_specs=VMEM,
        scratch_shapes=([pltpu.VMEM(ACC.shape, F32)] if last else []) + Chunk.shapes,
        compiler_params=pltpu.CompilerParams(vmem_limit_bytes=LIMIT),
        cost_estimate=cost(n * CUBIC_COST, n * 4 << 20),
        name="cubic_part",
    )(*args)


def payload_kernel(tiles, meta, out):
    out[:BODY, :] = tiles[...]
    top = jnp.full((8, B), 1e-30, F32)
    for t in range(SLOTS):
        v = jnp.abs(tiles[t * B : (t + 1) * B, :])
        top = jnp.maximum(top, jnp.max(v.reshape(B // 8, 8, B), 0))
    top = jnp.max(top, (0, 1), keepdims=True)
    row = lax.broadcasted_iota(jnp.int32, (8, B), 0)
    lane = lax.broadcasted_iota(jnp.int32, (8, B), 1)
    scales = jnp.where(lane == 0, TOP / top, top / TOP)
    out[BODY:, :] = jnp.where((row == 1) & (lane < 2), scales, meta[...])


def payload(tiles, meta):
    return pl.pallas_call(
        payload_kernel,
        out_shape=jax.ShapeDtypeStruct((BODY + 8, B), F32),
        in_specs=[VMEM, VMEM],
        out_specs=VMEM,
        compiler_params=pltpu.CompilerParams(vmem_limit_bytes=16 << 20),
        cost_estimate=pl.CostEstimate(flops=0, bytes_accessed=2 << 20, transcendentals=0),
        name="payload",
    )(tiles, meta)


def after(a, *others):
    return lax.optimization_barrier((a,) + others)[0]


def on_device(x_tiles, x_where, keep_where):
    r, c = lax.axis_index("row"), lax.axis_index("col")
    y, lo = r // 2, r % 2
    hi, x, core = c // 8, (c % 8) // 2, c % 2
    keep = keep_where[0, 0]
    own_where = x_where[0, 0]
    tiles = x_tiles[0, 0].reshape(BODY, B)
    meta = jnp.concatenate([own_where, keep]).astype(F32)
    own = payload(tiles, jnp.pad(meta[None], ((0, 7), (0, B - SLOTS - KEEP))))

    numbers = jnp.arange(N_ROW, dtype=jnp.int32)
    a_slot = jnp.array([0, 2, 6, 1, 3, 5, 7, 4], jnp.int32)[(numbers - x) % 4 + 4 * (numbers // 4 != hi)]
    b_slot = jnp.array([0, 2, 3, 1, 4, 6, 7, 5], jnp.int32)[(numbers // 2 - y) % 4 + 4 * (numbers % 2 != lo)]
    early = (a_slot < 4) & (b_slot < 5)
    then = (a_slot < 6) & (b_slot < 7) & ~early

    def listed(mask):
        mask = mask.astype(jnp.int32)
        hit = ((jnp.cumsum(mask) - 1)[None, :] == numbers[:, None]) & (mask[None, :] == 1)
        pick = jnp.stack([a_slot, b_slot], 1)
        lists = jnp.sum(jnp.where(hit[:, :, None], pick[None], 0), 1).reshape(-1)
        return jnp.concatenate([jnp.sum(mask)[None], core[None], lists]).astype(jnp.int32)

    by_b = jnp.sum(jnp.where(b_slot[None, :] == numbers[:, None], a_slot[None, :], 0), 1)
    ids = jnp.concatenate([core[None], by_b]).astype(jnp.int32)
    list1, list2, list3 = listed(early), listed(then), listed(~early & ~then)

    zh = send(own, "zh")
    xp, xm, yp, ym = send(own, "x+"), send(own, "x-"), send(own, "y+"), send(own, "y-")
    zh, xp, xm, own_z, ids, list1, list2, list3 = lax.optimization_barrier(
        (zh, xp, xm, own, ids, list1, list2, list3)
    )
    xhp, xhm = send(zh, "x+"), send(zh, "x-")
    zl = send(own_z, "zl")
    y2 = send(yp, "y+")
    zh_c, xp_c, xm_c, own_c = send(zh, "core"), send(xp, "core"), send(xm, "core"), send(own_z, "core")
    xhp, xhm, zl, y2, xp_t = lax.optimization_barrier((xhp, xhm, zl, y2, xp))
    yzp, yzm = send(zl, "y+"), send(zl, "y-")
    x2, xh2 = send(xp_t, "x+"), send(xhm, "x-")
    pairs = [(own_z, own_c), (xp, xp_c), (xm, xm_c), (zh, zh_c)]
    b_all = [own, yp, ym, y2, zl]
    acc = square_part(list1, pairs, b_all, None, chunks=2)
    yzp, yzm, x2, xh2, xhp, xhm, acc = lax.optimization_barrier((yzp, yzm, x2, xh2, xhp, xhm, acc))
    yz2 = send(yzp, "y+")
    xhp_c, xhm_c = send(xhp, "core"), send(xhm, "core")
    x2_c, xh2_c = send(x2, "core"), send(after(xh2, xhp_c), "core")
    pairs += [(xhp, xhp_c), (xhm, xhm_c)]
    b_all += [yzp, yzm]
    acc = square_part(list2, pairs, b_all, acc, chunks=2)
    pairs += [(x2, x2_c), (xh2, xh2_c)]
    b_all += [yz2]
    sq, s1, s2 = square_part(list3, pairs, b_all, acc, keep=keep, chunks=2)

    notes = [own, yp, ym, y2, zl, yzp, yzm, yz2]

    def add(slots, blocks, start, **kw):
        return cubic_part(ids, slots, pairs, [notes[j] for j in slots], blocks, start, **kw)

    def whole(a):
        return [(a, 0, KEEP)]

    def parted(one, *two):
        n = SECOND // len(two)
        return [(one, SECOND, FIRST)] + [(a, j * n, n) for j, a in enumerate(two)]

    cut, mid = SECOND * B, SECOND // 2 * B
    z_1 = send(s1, "zl")
    yp_s, ym_s = send(sq, "y+"), send(sq, "y-")
    acc = add([0], [whole(sq)], tiles, x_where=own_where)
    z_1, s2, acc = lax.optimization_barrier((z_1, s2, acc))
    z_2 = send(s2, "zl")
    yzp_1, yzm_1 = send(z_1, "y+"), send(z_1, "y-")
    acc = add([4], [parted(z_1, z_2)], acc)
    yp_s, ym_s, acc = lax.optimization_barrier((yp_s, ym_s, acc))
    yzp_2 = send(yp_s[:cut], "zl")
    y2_2a, y2_2b = send(yp_s[:mid], "y+"), send(ym_s[mid:cut], "y-")
    yp_1, ym_2 = yp_s[cut:], ym_s[:cut]
    acc = add([1], [whole(yp_s)], acc)
    yzp_1, yzm_1, y2_2a, y2_2b, yzp_2, yp_1, ym_2, acc = lax.optimization_barrier(
        (yzp_1, yzm_1, y2_2a, y2_2b, yzp_2, yp_1, ym_2, acc)
    )
    y2_1, yz2_1 = send(yp_1, "y+"), send(yzm_1, "y-")
    yzm_2 = send(ym_2, "zl")
    acc = add([2, 5], [whole(ym_s), parted(yzp_1, yzp_2)], acc)
    y2_2a, y2_2b, yzm_2, acc = lax.optimization_barrier((y2_2a, y2_2b, yzm_2, acc))
    yz2_2a, yz2_2b = send(y2_2a, "zl"), send(y2_2b, "zl")
    acc = add([6], [parted(yzm_1, yzm_2)], acc)
    out = add([3, 7], [parted(y2_1, y2_2a, y2_2b), parted(yz2_1, yz2_2a, yz2_2b)], acc, keep=keep)
    return out.reshape(1, 1, KEEP, B, B)


def solution(mesh):
    placed = (P("row", "col", None, None, None), P("row", "col", None), P("row", "col", None))
    return jax.shard_map(
        on_device,
        mesh=mesh,
        in_specs=placed,
        out_specs=P("row", "col", None, None, None),
        check_vma=False,
    )
```

```python
import functools

import jax
import jax.numpy as jnp
from jax import lax
from jax.experimental import pallas as pl
from jax.experimental.pallas import tpu as pltpu
from jax.sharding import PartitionSpec as P

B = 128
TC = 4
TR = 8
SLOTS = 12
KEEP = 24
N_ROW = 8
N_COL = 16
BODY = SLOTS * B
FIRST = 16
SECOND = KEEP - FIRST
LIMIT = 24 << 20

ANY = pl.BlockSpec(memory_space=pl.ANY)
VMEM = pl.BlockSpec(memory_space=pltpu.VMEM)
SMEM = pl.BlockSpec(memory_space=pltpu.SMEM)
F32 = jnp.float32
F8 = jnp.float8_e4m3fn
TOP = 240.0
REST = 256.0
CUBIC_COST = 1.0
BF16 = jnp.bfloat16


def decode(i):
    r, c = divmod(i, N_COL)
    return r // 2, (c // 8) * 2 + r % 2, (c % 8) // 2, c % 2


def encode(y, z, x, core):
    return ((y % 4) * 2 + z % 2) * N_COL + ((z // 2) * 4 + x % 4) * 2 + core


MOVES = {
    "y+": lambda y, z, x, k: (y + 1, z, x, k),
    "y-": lambda y, z, x, k: (y - 1, z, x, k),
    "x+": lambda y, z, x, k: (y, z, x + 1, k),
    "x-": lambda y, z, x, k: (y, z, x - 1, k),
    "zl": lambda y, z, x, k: (y, z ^ 1, x, k),
    "zh": lambda y, z, x, k: (y, z ^ 2, x, k),
    "core": lambda y, z, x, k: (y, z, x, 1 - k),
}


def send(a, move):
    pairs = [(i, encode(*MOVES[move](*decode(i)))) for i in range(N_ROW * N_COL)]
    return lax.ppermute(a, ("row", "col"), pairs)


def cost(chunks, moved):
    flops = chunks * 0.5 * 2 * (TR * B) * (TR * B) * (TC * B)
    return pl.CostEstimate(flops=int(flops), bytes_accessed=int(moved * 0.5 / 3), transcendentals=0)


def dot(a, b):
    return jnp.dot(a, b, preferred_element_type=F32)


def block_of(where):
    row = pl.multiple_of((where >> 2) * B, B)
    col = pl.multiple_of((where & 3) * B, B)
    return pl.ds(row, B), pl.ds(col, B)


def tile_of(t):
    return pl.ds(pl.multiple_of(t * B, B), B)


def split(v, scale):
    hi = v.astype(BF16)
    wide = hi.astype(F32)
    return hi, (wide * scale).astype(F8), ((v - wide) * scale * REST).astype(F8)


class Chunk:
    def __init__(self, refs):
        self.raw, self.meta, self.braw, self.bmeta = refs[:4]
        self.a, self.b = refs[4:7], refs[7:10]
        self.sem, self.bsem, self.asem = refs[10:]

    shapes = [
        pltpu.VMEM((2, 2, BODY, B), F32),
        pltpu.SMEM((2, 2, 8, B), F32),
        pltpu.VMEM((2, KEEP * B, B), F32),
        pltpu.SMEM((2, 8, B), F32),
        pltpu.VMEM((TR * B, TR * B), BF16),
        pltpu.VMEM((TR * B, TR * B), F8),
        pltpu.VMEM((TR * B, TR * B), F8),
        pltpu.VMEM((TR * B, TC * B), BF16),
        pltpu.VMEM((TR * B, TC * B), F8),
        pltpu.VMEM((TR * B, TC * B), F8),
        pltpu.SemaphoreType.DMA((2, 4)),
        pltpu.SemaphoreType.DMA((2, 4)),
        pltpu.SemaphoreType.DMA,
    ]

    def clear(self):
        for ref in self.a + self.b:
            ref[...] = jnp.zeros(ref.shape, ref.dtype)

    def fetch(self, slot, which, core, pairs):
        def start(ref, half):
            pltpu.make_async_copy(
                ref.at[pl.ds(0, BODY), :], self.raw.at[slot, half], self.sem.at[slot, half]
            ).start()
            pltpu.make_async_copy(
                ref.at[pl.ds(BODY, 8), :], self.meta.at[slot, half], self.sem.at[slot, 2 + half]
            ).start()

        for j, (own, other) in enumerate(pairs):

            @pl.when(which == j)
            def _():
                start(own, core)
                start(other, 1 - core)

    def arrive(self, slot, ref):
        for half in range(2):
            pltpu.make_async_copy(
                ref.at[pl.ds(0, BODY), :], self.raw.at[slot, half], self.sem.at[slot, half]
            ).wait()
            pltpu.make_async_copy(
                ref.at[pl.ds(BODY, 8), :], self.meta.at[slot, half], self.sem.at[slot, 2 + half]
            ).wait()

    def piece(self, slot, ref, start, at, rows, sem):
        return pltpu.make_async_copy(
            ref.at[pl.ds(start, rows), :], self.braw.at[slot, pl.ds(at, rows), :], self.bsem.at[slot, sem]
        )

    def note(self, slot, ref, start):
        return pltpu.make_async_copy(ref.at[pl.ds(start, 8), :], self.bmeta.at[slot], self.bsem.at[slot, 3])

    def each_a(self, slot, put):
        for half in range(2):

            @pl.loop(0, SLOTS, unroll=4)
            def _(t):
                where = self.meta[slot, half, 0, t].astype(jnp.int32)
                row = pl.ds(pl.multiple_of((where >> 2) * B, B), B)
                col = pl.ds(pl.multiple_of(((where & 3) + TC * half) * B, B), B)
                put((row, col), half, t)

    def load_a(self, slot):
        scale = jnp.minimum(self.meta[slot, 0, 1, 0], self.meta[slot, 1, 1, 0])

        def put(at, half, t):
            for ref, v in zip(self.a, split(self.raw[slot, half, tile_of(t), :], scale)):
                ref[at] = v

        self.each_a(slot, put)
        return jnp.maximum(self.meta[slot, 0, 1, 1], self.meta[slot, 1, 1, 1])

    def wipe_a(self, slot):
        def put(at, half, t):
            for ref in self.a:
                ref[at] = jnp.zeros((B, B), ref.dtype)

        self.each_a(slot, put)

    def load_b(self, slot, n, lane, measured):
        if measured:
            top = jnp.full((8, B), 1e-30, F32)
            for t in range(n):
                v = jnp.abs(self.braw[slot, t * B : (t + 1) * B, :])
                top = jnp.maximum(top, jnp.max(v.reshape(B // 8, 8, B), 0))
            top = jnp.max(top, (0, 1), keepdims=True)
            scale, back = TOP / top, top / TOP
        else:
            scale, back = self.bmeta[slot, 1, 0], self.bmeta[slot, 1, 1]

        @pl.loop(0, n, unroll=4)
        def _(t):
            at = block_of(self.bmeta[slot, 0, lane + t].astype(jnp.int32))
            for ref, v in zip(self.b, split(self.braw[slot, tile_of(t), :], scale)):
                ref[at] = v

        return back

    def wipe_b(self, slot, n, lane):
        @pl.loop(0, n, unroll=4)
        def _(t):
            at = block_of(self.bmeta[slot, 0, lane + t].astype(jnp.int32))
            for ref in self.b:
                ref[at] = jnp.zeros((B, B), ref.dtype)

    def multiply(self, acc, back):
        ah, ah8, al8 = self.a
        for jp in range(2):
            cols = slice(jp * 2 * B, (jp + 1) * 2 * B)
            bh, bh8, bl8 = (ref[:, cols] for ref in self.b)
            small = dot(al8[...], bh8) + dot(ah8[...], bl8)
            acc[:, cols] = acc[:, cols] + (dot(ah[...], bh) + small * back)


def pack(acc, keep, start, n, out, scale=None):
    @pl.loop(0, n, unroll=4)
    def _(t):
        v = acc[block_of(keep[start + t])]
        out[tile_of(t), :] = v if scale is None else scale * v


def square_kernel(n_pair, cuts, first, last, *refs):
    refs = list(refs)
    ids = refs.pop(0)
    pairs = [(refs.pop(0), refs.pop(0)) for _ in range(n_pair)]
    bs = [[refs.pop(0) for _ in range(n)] for n in cuts]
    acc_in = None if first else refs.pop(0)
    if last:
        keep, out, out1, out2, acc = (refs.pop(0) for _ in range(5))
    else:
        acc = refs.pop(0)
    chunk = Chunk(refs)
    count, core = ids[0], ids[1]

    def fetch(t):
        slot = lax.rem(t, 2)
        chunk.fetch(slot, ids[2 + 2 * t], core, pairs)
        for j, parts in enumerate(bs):

            @pl.when(ids[3 + 2 * t] == j)
            def _():
                rows = BODY // len(parts)
                for k in range(2):
                    start = BODY // 2 * k if len(parts) == 1 else 0
                    chunk.piece(slot, parts[k * (len(parts) - 1)], start, BODY // 2 * k, BODY // 2, k).start()
                chunk.note(slot, parts[-1], rows).start()

    @pl.when(count > 0)
    def _():
        fetch(jnp.int32(0))

    if not first:
        pltpu.make_async_copy(acc_in, acc, chunk.asem).start()
    chunk.clear()
    if first:
        acc[...] = jnp.zeros(acc.shape, F32)

    @pl.loop(0, count)
    def _(t):
        slot = lax.rem(t, 2)

        @pl.when(t + 1 < count)
        def _():
            fetch(t + 1)

        chunk.arrive(slot, pairs[0][0])
        for k in range(2):
            chunk.piece(slot, bs[0][0], 0, BODY // 2 * k, BODY // 2, k).wait()
        chunk.note(slot, bs[0][0], 0).wait()
        back = chunk.load_a(slot) * chunk.load_b(slot, SLOTS, 0, False) * (1.0 / REST)
        if not first:

            @pl.when(t == 0)
            def _():
                pltpu.make_async_copy(acc_in, acc, chunk.asem).wait()

        chunk.multiply(acc, back)

        @pl.when(t + 1 < count)
        def _():
            chunk.wipe_a(slot)
            chunk.wipe_b(slot, SLOTS, 0)

    if not first:

        @pl.when(count == 0)
        def _():
            pltpu.make_async_copy(acc_in, acc, chunk.asem).wait()

    if last:
        pack(acc, keep, 0, KEEP, out)
        pack(acc, keep, SECOND, FIRST, out1)
        pack(acc, keep, 0, SECOND, out2)


ACC = jax.ShapeDtypeStruct((TR * B, TC * B), F32)


def square_part(ids, pairs, bs, acc, keep=None, chunks=3):
    last = keep is not None
    args = [ids] + [p for pair in pairs for p in pair] + [p for parts in bs for p in parts]
    specs = [SMEM] + [ANY] * (len(args) - 1)
    if acc is not None:
        args.append(acc)
        specs.append(ANY)
    if last:
        args.append(keep)
        specs.append(SMEM)
    packed = (
        jax.ShapeDtypeStruct((KEEP * B, B), F32),
        jax.ShapeDtypeStruct((FIRST * B, B), F32),
        jax.ShapeDtypeStruct((SECOND * B, B), F32),
    )
    return pl.pallas_call(
        functools.partial(square_kernel, len(pairs), [len(p) for p in bs], acc is None, last),
        out_shape=packed if last else ACC,
        in_specs=specs,
        out_specs=(VMEM,) * 3 if last else VMEM,
        scratch_shapes=([pltpu.VMEM(ACC.shape, F32)] if last else []) + Chunk.shapes,
        compiler_params=pltpu.CompilerParams(vmem_limit_bytes=LIMIT),
        cost_estimate=cost(chunks, chunks * 4 << 20),
        name="square_part",
    )(*args)


def cubic_kernel(slots, groups, n_pair, head, last, *refs):
    refs = list(refs)
    ids = refs.pop(0)
    pairs = [(refs.pop(0), refs.pop(0)) for _ in range(n_pair)]
    notes = [refs.pop(0) for _ in slots]
    pieces = [[refs.pop(0) for _ in group] for group in groups]
    start = refs.pop(0)
    where_x = refs.pop(0) if head else None
    if last:
        keep, out, acc = refs.pop(0), refs.pop(0), refs.pop(0)
    else:
        acc = refs.pop(0)
    chunk = Chunk(refs)
    core = ids[0]

    def fetch(s):
        chunk.fetch(s % 2, ids[1 + slots[s]], core, pairs)
        copies = [
            chunk.piece(s % 2, ref, 0, at * B, n * B, j)
            for j, (ref, (at, n)) in enumerate(zip(pieces[s], groups[s]))
        ]
        copies.append(chunk.note(s % 2, notes[s], notes[s].shape[0] - 8))
        for cp in copies:
            cp.start()
        return copies

    loads = fetch(0)
    if not head:
        pltpu.make_async_copy(start, acc, chunk.asem).start()
    chunk.clear()
    if head:
        acc[...] = jnp.zeros(acc.shape, F32)

        @pl.loop(0, SLOTS)
        def _(t):
            acc[block_of(where_x[t])] = -3.0 * start[tile_of(t), :]

    for s in range(len(slots)):
        following = fetch(s + 1) if s + 1 < len(slots) else None
        for cp in loads:
            cp.wait()
        loads = following
        back = chunk.load_b(s % 2, KEEP, SLOTS, True)
        chunk.arrive(s % 2, pairs[0][0])
        back = back * (chunk.load_a(s % 2) * (1.0 / REST))
        if s == 0 and not head:
            pltpu.make_async_copy(start, acc, chunk.asem).wait()
        chunk.multiply(acc, back)
        if s + 1 < len(slots):
            chunk.wipe_a(s % 2)
            chunk.wipe_b(s % 2, KEEP, SLOTS)
    if last:
        pack(acc, keep, 0, KEEP, out, -0.5)


def cubic_part(ids, slots, pairs, notes, blocks, start, x_where=None, keep=None):
    head, last = x_where is not None, keep is not None
    groups = [[(at, n) for _, at, n in group] for group in blocks]
    args = [ids] + [p for pair in pairs for p in pair] + list(notes)
    args += [ref for group in blocks for ref, _, _ in group]
    specs = [SMEM] + [ANY] * (len(args) - 1)
    args.append(start)
    specs.append(VMEM if head else ANY)
    for extra in (x_where, keep):
        if extra is not None:
            args.append(extra)
            specs.append(SMEM)
    n = len(blocks)
    return pl.pallas_call(
        functools.partial(cubic_kernel, slots, groups, len(pairs), head, last),
        out_shape=jax.ShapeDtypeStruct((KEEP * B, B), F32) if last else ACC,
        in_specs=specs,
        out_specs=VMEM,
        scratch_shapes=([pltpu.VMEM(ACC.shape, F32)] if last else []) + Chunk.shapes,
        compiler_params=pltpu.CompilerParams(vmem_limit_bytes=LIMIT),
        cost_estimate=cost(n * CUBIC_COST, n * 4 << 20),
        name="cubic_part",
    )(*args)


def payload_kernel(tiles, meta, out):
    out[:BODY, :] = tiles[...]
    top = jnp.full((8, B), 1e-30, F32)
    for t in range(SLOTS):
        v = jnp.abs(tiles[t * B : (t + 1) * B, :])
        top = jnp.maximum(top, jnp.max(v.reshape(B // 8, 8, B), 0))
    top = jnp.max(top, (0, 1), keepdims=True)
    row = lax.broadcasted_iota(jnp.int32, (8, B), 0)
    lane = lax.broadcasted_iota(jnp.int32, (8, B), 1)
    scales = jnp.where(lane == 0, TOP / top, top / TOP)
    out[BODY:, :] = jnp.where((row == 1) & (lane < 2), scales, meta[...])


def payload(tiles, meta):
    return pl.pallas_call(
        payload_kernel,
        out_shape=jax.ShapeDtypeStruct((BODY + 8, B), F32),
        in_specs=[VMEM, VMEM],
        out_specs=VMEM,
        compiler_params=pltpu.CompilerParams(vmem_limit_bytes=16 << 20),
        cost_estimate=pl.CostEstimate(flops=0, bytes_accessed=2 << 20, transcendentals=0),
        name="payload",
    )(tiles, meta)


def after(a, *others):
    return lax.optimization_barrier((a,) + others)[0]


def on_device(x_tiles, x_where, keep_where):
    r, c = lax.axis_index("row"), lax.axis_index("col")
    y, lo = r // 2, r % 2
    hi, x, core = c // 8, (c % 8) // 2, c % 2
    keep = keep_where[0, 0]
    own_where = x_where[0, 0]
    tiles = x_tiles[0, 0].reshape(BODY, B)
    meta = jnp.concatenate([own_where, keep]).astype(F32)
    own = payload(tiles, jnp.pad(meta[None], ((0, 7), (0, B - SLOTS - KEEP))))

    numbers = jnp.arange(N_ROW, dtype=jnp.int32)
    a_slot = jnp.array([0, 2, 6, 1, 3, 5, 7, 4], jnp.int32)[(numbers - x) % 4 + 4 * (numbers // 4 != hi)]
    b_slot = jnp.array([0, 2, 3, 1, 4, 6, 7, 5], jnp.int32)[(numbers // 2 - y) % 4 + 4 * (numbers % 2 != lo)]
    early = (a_slot < 4) & (b_slot < 5)
    then = (a_slot < 6) & (b_slot < 7) & ~early

    def listed(mask):
        mask = mask.astype(jnp.int32)
        hit = ((jnp.cumsum(mask) - 1)[None, :] == numbers[:, None]) & (mask[None, :] == 1)
        pick = jnp.stack([a_slot, b_slot], 1)
        lists = jnp.sum(jnp.where(hit[:, :, None], pick[None], 0), 1).reshape(-1)
        return jnp.concatenate([jnp.sum(mask)[None], core[None], lists]).astype(jnp.int32)

    by_b = jnp.sum(jnp.where(b_slot[None, :] == numbers[:, None], a_slot[None, :], 0), 1)
    ids = jnp.concatenate([core[None], by_b]).astype(jnp.int32)
    list1, list2, list3 = listed(early), listed(then), listed(~early & ~then)

    zh = send(own, "zh")
    xp, xm, yp, ym = send(own, "x+"), send(own, "x-"), send(own, "y+"), send(own, "y-")
    zh, xp, xm, own_z, ids, list1, list2, list3 = lax.optimization_barrier(
        (zh, xp, xm, own, ids, list1, list2, list3)
    )
    xhp, xhm = send(zh, "x+"), send(zh, "x-")
    zl = send(own_z, "zl")
    y2 = send(yp, "y+")
    zh_c, xp_c, xm_c, own_c = send(zh, "core"), send(xp, "core"), send(xm, "core"), send(own_z, "core")
    xhp, xhm, zl, y2, xp_t = lax.optimization_barrier((xhp, xhm, zl, y2, xp))
    yzp, yzm = send(zl, "y+"), send(zl, "y-")
    x2, xh2 = send(xp_t, "x+"), send(xhm, "x-")
    pairs = [(own_z, own_c), (xp, xp_c), (xm, xm_c), (zh, zh_c)]
    b_all = [[own], [yp], [ym], [y2], [zl]]
    acc = square_part(list1, pairs, b_all, None, chunks=2)
    yzp, yzm, x2, xh2, xhp, xhm, acc = lax.optimization_barrier((yzp, yzm, x2, xh2, xhp, xhm, acc))
    half = BODY // 2
    yz2 = [send(yzp[:half], "y+"), send(yzm[half:], "y-")]
    xhp_c, xhm_c = send(xhp, "core"), send(xhm, "core")
    x2_c, xh2_c = send(x2, "core"), send(after(xh2, xhp_c), "core")
    pairs += [(xhp, xhp_c), (xhm, xhm_c)]
    b_all += [[yzp], [yzm]]
    acc = square_part(list2, pairs, b_all, acc, chunks=2)
    pairs += [(x2, x2_c), (xh2, xh2_c)]
    b_all += [yz2]
    sq, s1, s2 = square_part(list3, pairs, b_all, acc, keep=keep, chunks=2)

    notes = [own, yp, ym, y2, zl, yzp, yzm, yz2[1]]

    def add(slots, blocks, start, **kw):
        return cubic_part(ids, slots, pairs, [notes[j] for j in slots], blocks, start, **kw)

    def whole(a):
        return [(a, 0, KEEP)]

    def parted(one, *two):
        n = SECOND // len(two)
        return [(one, SECOND, FIRST)] + [(a, j * n, n) for j, a in enumerate(two)]

    cut, mid = SECOND * B, SECOND // 2 * B
    z_1 = send(s1, "zl")
    yp_s, ym_s = send(sq, "y+"), send(sq, "y-")
    acc = add([0], [whole(sq)], tiles, x_where=own_where)
    z_1, s2, acc = lax.optimization_barrier((z_1, s2, acc))
    z_2 = send(s2, "zl")
    yzp_1, yzm_1 = send(z_1, "y+"), send(z_1, "y-")
    acc = add([4], [parted(z_1, z_2)], acc)
    yp_s, ym_s, acc = lax.optimization_barrier((yp_s, ym_s, acc))
    yzp_2 = send(yp_s[:cut], "zl")
    y2_2a, y2_2b = send(yp_s[:mid], "y+"), send(ym_s[mid:cut], "y-")
    yp_1, ym_2 = yp_s[cut:], ym_s[:cut]
    acc = add([1], [whole(yp_s)], acc)
    ym_2, yzp_2, acc = lax.optimization_barrier((ym_2, yzp_2, acc))
    yzm_2 = send(ym_2, "zl")
    yzp_1, yzm_1, y2_2a, y2_2b, yp_1, acc = lax.optimization_barrier((yzp_1, yzm_1, y2_2a, y2_2b, yp_1, acc))
    y2_1, yz2_1 = send(yp_1, "y+"), send(yzm_1, "y-")
    acc = add([2, 5], [whole(ym_s), parted(yzp_1, yzp_2)], acc)
    y2_2a, y2_2b, yzm_2, acc = lax.optimization_barrier((y2_2a, y2_2b, yzm_2, acc))
    yz2_2a, yz2_2b = send(y2_2a, "zl"), send(y2_2b, "zl")
    acc = add([6], [parted(yzm_1, yzm_2)], acc)
    out = add([3, 7], [parted(y2_1, y2_2a, y2_2b), parted(yz2_1, yz2_2a, yz2_2b)], acc, keep=keep)
    return out.reshape(1, 1, KEEP, B, B)


def solution(mesh):
    placed = (P("row", "col", None, None, None), P("row", "col", None), P("row", "col", None))
    return jax.shard_map(
        on_device,
        mesh=mesh,
        in_specs=placed,
        out_specs=P("row", "col", None, None, None),
        check_vma=False,
    )
```

```python
import functools

import jax
import jax.numpy as jnp
from jax import lax
from jax.experimental import pallas as pl
from jax.experimental.pallas import tpu as pltpu
from jax.sharding import PartitionSpec as P

B = 128
TC = 4
TR = 8
SLOTS = 12
KEEP = 24
N_ROW = 8
N_COL = 16
BODY = SLOTS * B
FIRST = 16
SECOND = KEEP - FIRST
LIMIT = 24 << 20

ANY = pl.BlockSpec(memory_space=pl.ANY)
VMEM = pl.BlockSpec(memory_space=pltpu.VMEM)
SMEM = pl.BlockSpec(memory_space=pltpu.SMEM)
F32 = jnp.float32
F8 = jnp.float8_e4m3fn
TOP = 240.0
REST = 256.0
CUBIC_COST = 1.0
BF16 = jnp.bfloat16


def decode(i):
    r, c = divmod(i, N_COL)
    return r // 2, (c // 8) * 2 + r % 2, (c % 8) // 2, c % 2


def encode(y, z, x, core):
    return ((y % 4) * 2 + z % 2) * N_COL + ((z // 2) * 4 + x % 4) * 2 + core


MOVES = {
    "y+": lambda y, z, x, k: (y + 1, z, x, k),
    "y-": lambda y, z, x, k: (y - 1, z, x, k),
    "x+": lambda y, z, x, k: (y, z, x + 1, k),
    "x-": lambda y, z, x, k: (y, z, x - 1, k),
    "zl": lambda y, z, x, k: (y, z ^ 1, x, k),
    "zh": lambda y, z, x, k: (y, z ^ 2, x, k),
    "core": lambda y, z, x, k: (y, z, x, 1 - k),
}


def send(a, move):
    pairs = [(i, encode(*MOVES[move](*decode(i)))) for i in range(N_ROW * N_COL)]
    return lax.ppermute(a, ("row", "col"), pairs)


def cost(chunks, moved):
    flops = chunks * 0.5 * 2 * (TR * B) * (TR * B) * (TC * B)
    return pl.CostEstimate(flops=int(flops), bytes_accessed=int(moved * 0.5 / 3), transcendentals=0)


def dot(a, b):
    return jnp.dot(a, b, preferred_element_type=F32)


def block_of(where):
    row = pl.multiple_of((where >> 2) * B, B)
    col = pl.multiple_of((where & 3) * B, B)
    return pl.ds(row, B), pl.ds(col, B)


def tile_of(t):
    return pl.ds(pl.multiple_of(t * B, B), B)


def split(v, scale):
    hi = v.astype(BF16)
    wide = hi.astype(F32)
    return hi, (wide * scale).astype(F8), ((v - wide) * scale * REST).astype(F8)


class Chunk:
    def __init__(self, refs):
        self.raw, self.meta, self.braw, self.bmeta = refs[:4]
        self.a, self.b = refs[4:7], refs[7:10]
        self.sem, self.bsem, self.asem = refs[10:]

    shapes = [
        pltpu.VMEM((2, 2, BODY, B), F32),
        pltpu.SMEM((2, 2, 8, B), F32),
        pltpu.VMEM((2, KEEP * B, B), F32),
        pltpu.SMEM((2, 8, B), F32),
        pltpu.VMEM((TR * B, TR * B), BF16),
        pltpu.VMEM((TR * B, TR * B), F8),
        pltpu.VMEM((TR * B, TR * B), F8),
        pltpu.VMEM((TR * B, TC * B), BF16),
        pltpu.VMEM((TR * B, TC * B), F8),
        pltpu.VMEM((TR * B, TC * B), F8),
        pltpu.SemaphoreType.DMA((2, 4)),
        pltpu.SemaphoreType.DMA((2, 4)),
        pltpu.SemaphoreType.DMA,
    ]

    def clear(self):
        for ref in self.a + self.b:
            ref[...] = jnp.zeros(ref.shape, ref.dtype)

    def fetch(self, slot, which, core, pairs):
        def start(ref, half):
            pltpu.make_async_copy(
                ref.at[pl.ds(0, BODY), :], self.raw.at[slot, half], self.sem.at[slot, half]
            ).start()
            pltpu.make_async_copy(
                ref.at[pl.ds(BODY, 8), :], self.meta.at[slot, half], self.sem.at[slot, 2 + half]
            ).start()

        for j, (own, other) in enumerate(pairs):

            @pl.when(which == j)
            def _():
                start(own, core)
                start(other, 1 - core)

    def arrive(self, slot, ref):
        for half in range(2):
            pltpu.make_async_copy(
                ref.at[pl.ds(0, BODY), :], self.raw.at[slot, half], self.sem.at[slot, half]
            ).wait()
            pltpu.make_async_copy(
                ref.at[pl.ds(BODY, 8), :], self.meta.at[slot, half], self.sem.at[slot, 2 + half]
            ).wait()

    def piece(self, slot, ref, start, at, rows, sem):
        return pltpu.make_async_copy(
            ref.at[pl.ds(start, rows), :], self.braw.at[slot, pl.ds(at, rows), :], self.bsem.at[slot, sem]
        )

    def note(self, slot, ref, start):
        return pltpu.make_async_copy(ref.at[pl.ds(start, 8), :], self.bmeta.at[slot], self.bsem.at[slot, 3])

    def each_a(self, slot, put):
        for half in range(2):

            @pl.loop(0, SLOTS, unroll=4)
            def _(t):
                where = self.meta[slot, half, 0, t].astype(jnp.int32)
                row = pl.ds(pl.multiple_of((where >> 2) * B, B), B)
                col = pl.ds(pl.multiple_of(((where & 3) + TC * half) * B, B), B)
                put((row, col), half, t)

    def load_a(self, slot):
        scale = jnp.minimum(self.meta[slot, 0, 1, 0], self.meta[slot, 1, 1, 0])

        def put(at, half, t):
            for ref, v in zip(self.a, split(self.raw[slot, half, tile_of(t), :], scale)):
                ref[at] = v

        self.each_a(slot, put)
        return jnp.maximum(self.meta[slot, 0, 1, 1], self.meta[slot, 1, 1, 1])

    def wipe_a(self, slot):
        def put(at, half, t):
            for ref in self.a:
                ref[at] = jnp.zeros((B, B), ref.dtype)

        self.each_a(slot, put)

    def load_b(self, slot, n, lane, measured):
        if measured:
            top = jnp.full((8, B), 1e-30, F32)
            for t in range(n):
                v = jnp.abs(self.braw[slot, t * B : (t + 1) * B, :])
                top = jnp.maximum(top, jnp.max(v.reshape(B // 8, 8, B), 0))
            top = jnp.max(top, (0, 1), keepdims=True)
            scale, back = TOP / top, top / TOP
        else:
            scale, back = self.bmeta[slot, 1, 0], self.bmeta[slot, 1, 1]

        @pl.loop(0, n, unroll=4)
        def _(t):
            at = block_of(self.bmeta[slot, 0, lane + t].astype(jnp.int32))
            for ref, v in zip(self.b, split(self.braw[slot, tile_of(t), :], scale)):
                ref[at] = v

        return back

    def wipe_b(self, slot, n, lane):
        @pl.loop(0, n, unroll=4)
        def _(t):
            at = block_of(self.bmeta[slot, 0, lane + t].astype(jnp.int32))
            for ref in self.b:
                ref[at] = jnp.zeros((B, B), ref.dtype)

    def multiply(self, acc, back):
        ah, ah8, al8 = self.a
        for jp in range(2):
            cols = slice(jp * 2 * B, (jp + 1) * 2 * B)
            bh, bh8, bl8 = (ref[:, cols] for ref in self.b)
            small = dot(al8[...], bh8) + dot(ah8[...], bl8)
            acc[:, cols] = acc[:, cols] + (dot(ah[...], bh) + small * back)


def pack(acc, keep, start, n, out, scale=None):
    @pl.loop(0, n, unroll=4)
    def _(t):
        v = acc[block_of(keep[start + t])]
        out[tile_of(t), :] = v if scale is None else scale * v


def square_kernel(n_pair, cuts, first, last, *refs):
    refs = list(refs)
    ids = refs.pop(0)
    pairs = [(refs.pop(0), refs.pop(0)) for _ in range(n_pair)]
    bs = [[refs.pop(0) for _ in range(n)] for n in cuts]
    acc_in = None if first else refs.pop(0)
    if last:
        keep, out, out1, out2, acc = (refs.pop(0) for _ in range(5))
    else:
        acc = refs.pop(0)
    chunk = Chunk(refs)
    count, core = ids[0], ids[1]

    def fetch(t):
        slot = lax.rem(t, 2)
        chunk.fetch(slot, ids[2 + 2 * t], core, pairs)
        for j, parts in enumerate(bs):

            @pl.when(ids[3 + 2 * t] == j)
            def _():
                rows = BODY // len(parts)
                for k in range(2):
                    start = BODY // 2 * k if len(parts) == 1 else 0
                    chunk.piece(slot, parts[k * (len(parts) - 1)], start, BODY // 2 * k, BODY // 2, k).start()
                chunk.note(slot, parts[-1], rows).start()

    @pl.when(count > 0)
    def _():
        fetch(jnp.int32(0))

    if not first:
        pltpu.make_async_copy(acc_in, acc, chunk.asem).start()
    chunk.clear()
    if first:
        acc[...] = jnp.zeros(acc.shape, F32)

    @pl.loop(0, count)
    def _(t):
        slot = lax.rem(t, 2)

        @pl.when(t + 1 < count)
        def _():
            fetch(t + 1)

        chunk.arrive(slot, pairs[0][0])
        for k in range(2):
            chunk.piece(slot, bs[0][0], 0, BODY // 2 * k, BODY // 2, k).wait()
        chunk.note(slot, bs[0][0], 0).wait()
        back = chunk.load_a(slot) * chunk.load_b(slot, SLOTS, 0, False) * (1.0 / REST)
        if not first:

            @pl.when(t == 0)
            def _():
                pltpu.make_async_copy(acc_in, acc, chunk.asem).wait()

        chunk.multiply(acc, back)

        @pl.when(t + 1 < count)
        def _():
            chunk.wipe_a(slot)
            chunk.wipe_b(slot, SLOTS, 0)

    if not first:

        @pl.when(count == 0)
        def _():
            pltpu.make_async_copy(acc_in, acc, chunk.asem).wait()

    if last:
        pack(acc, keep, 0, KEEP, out)
        pack(acc, keep, SECOND, FIRST, out1)
        pack(acc, keep, 0, SECOND, out2)


ACC = jax.ShapeDtypeStruct((TR * B, TC * B), F32)


def square_part(ids, pairs, bs, acc, keep=None, chunks=3):
    last = keep is not None
    args = [ids] + [p for pair in pairs for p in pair] + [p for parts in bs for p in parts]
    specs = [SMEM] + [ANY] * (len(args) - 1)
    if acc is not None:
        args.append(acc)
        specs.append(ANY)
    if last:
        args.append(keep)
        specs.append(SMEM)
    packed = (
        jax.ShapeDtypeStruct((KEEP * B, B), F32),
        jax.ShapeDtypeStruct((FIRST * B, B), F32),
        jax.ShapeDtypeStruct((SECOND * B, B), F32),
    )
    return pl.pallas_call(
        functools.partial(square_kernel, len(pairs), [len(p) for p in bs], acc is None, last),
        out_shape=packed if last else ACC,
        in_specs=specs,
        out_specs=(VMEM,) * 3 if last else VMEM,
        scratch_shapes=([pltpu.VMEM(ACC.shape, F32)] if last else []) + Chunk.shapes,
        compiler_params=pltpu.CompilerParams(vmem_limit_bytes=LIMIT),
        cost_estimate=cost(chunks, chunks * 4 << 20),
        name="square_part",
    )(*args)


def cubic_kernel(slots, groups, n_pair, head, last, *refs):
    refs = list(refs)
    ids = refs.pop(0)
    pairs = [(refs.pop(0), refs.pop(0)) for _ in range(n_pair)]
    notes = [refs.pop(0) for _ in slots]
    pieces = [[refs.pop(0) for _ in group] for group in groups]
    start = refs.pop(0)
    where_x = refs.pop(0) if head else None
    if last:
        keep, out, acc = refs.pop(0), refs.pop(0), refs.pop(0)
    else:
        acc = refs.pop(0)
    chunk = Chunk(refs)
    core = ids[0]

    def fetch(s):
        chunk.fetch(s % 2, ids[1 + slots[s]], core, pairs)
        copies = [
            chunk.piece(s % 2, ref, 0, at * B, n * B, j)
            for j, (ref, (at, n)) in enumerate(zip(pieces[s], groups[s]))
        ]
        copies.append(chunk.note(s % 2, notes[s], notes[s].shape[0] - 8))
        for cp in copies:
            cp.start()
        return copies

    loads = fetch(0)
    if not head:
        pltpu.make_async_copy(start, acc, chunk.asem).start()
    chunk.clear()
    if head:
        acc[...] = jnp.zeros(acc.shape, F32)

        @pl.loop(0, SLOTS)
        def _(t):
            acc[block_of(where_x[t])] = -3.0 * start[tile_of(t), :]

    for s in range(len(slots)):
        following = fetch(s + 1) if s + 1 < len(slots) else None
        for cp in loads:
            cp.wait()
        loads = following
        back = chunk.load_b(s % 2, KEEP, SLOTS, True)
        chunk.arrive(s % 2, pairs[0][0])
        back = back * (chunk.load_a(s % 2) * (1.0 / REST))
        if s == 0 and not head:
            pltpu.make_async_copy(start, acc, chunk.asem).wait()
        chunk.multiply(acc, back)
        if s + 1 < len(slots):
            chunk.wipe_a(s % 2)
            chunk.wipe_b(s % 2, KEEP, SLOTS)
    if last:
        pack(acc, keep, 0, KEEP, out, -0.5)


def cubic_part(ids, slots, pairs, notes, blocks, start, x_where=None, keep=None):
    head, last = x_where is not None, keep is not None
    groups = [[(at, n) for _, at, n in group] for group in blocks]
    args = [ids] + [p for pair in pairs for p in pair] + list(notes)
    args += [ref for group in blocks for ref, _, _ in group]
    specs = [SMEM] + [ANY] * (len(args) - 1)
    args.append(start)
    specs.append(VMEM if head else ANY)
    for extra in (x_where, keep):
        if extra is not None:
            args.append(extra)
            specs.append(SMEM)
    n = len(blocks)
    return pl.pallas_call(
        functools.partial(cubic_kernel, slots, groups, len(pairs), head, last),
        out_shape=jax.ShapeDtypeStruct((KEEP * B, B), F32) if last else ACC,
        in_specs=specs,
        out_specs=VMEM,
        scratch_shapes=([pltpu.VMEM(ACC.shape, F32)] if last else []) + Chunk.shapes,
        compiler_params=pltpu.CompilerParams(vmem_limit_bytes=LIMIT),
        cost_estimate=cost(n * CUBIC_COST, n * 4 << 20),
        name="cubic_part",
    )(*args)


def payload_kernel(tiles, meta, out):
    out[:BODY, :] = tiles[...]
    top = jnp.full((8, B), 1e-30, F32)
    for t in range(SLOTS):
        v = jnp.abs(tiles[t * B : (t + 1) * B, :])
        top = jnp.maximum(top, jnp.max(v.reshape(B // 8, 8, B), 0))
    top = jnp.max(top, (0, 1), keepdims=True)
    row = lax.broadcasted_iota(jnp.int32, (8, B), 0)
    lane = lax.broadcasted_iota(jnp.int32, (8, B), 1)
    scales = jnp.where(lane == 0, TOP / top, top / TOP)
    out[BODY:, :] = jnp.where((row == 1) & (lane < 2), scales, meta[...])


def payload(tiles, meta):
    return pl.pallas_call(
        payload_kernel,
        out_shape=jax.ShapeDtypeStruct((BODY + 8, B), F32),
        in_specs=[VMEM, VMEM],
        out_specs=VMEM,
        compiler_params=pltpu.CompilerParams(vmem_limit_bytes=16 << 20),
        cost_estimate=pl.CostEstimate(flops=0, bytes_accessed=2 << 20, transcendentals=0),
        name="payload",
    )(tiles, meta)


def after(a, *others):
    return lax.optimization_barrier((a,) + others)[0]


def on_device(x_tiles, x_where, keep_where):
    r, c = lax.axis_index("row"), lax.axis_index("col")
    y, lo = r // 2, r % 2
    hi, x, core = c // 8, (c % 8) // 2, c % 2
    keep = keep_where[0, 0]
    own_where = x_where[0, 0]
    tiles = x_tiles[0, 0].reshape(BODY, B)
    meta = jnp.concatenate([own_where, keep]).astype(F32)
    own = payload(tiles, jnp.pad(meta[None], ((0, 7), (0, B - SLOTS - KEEP))))

    numbers = jnp.arange(N_ROW, dtype=jnp.int32)
    a_slot = jnp.array([0, 2, 6, 1, 3, 5, 7, 4], jnp.int32)[(numbers - x) % 4 + 4 * (numbers // 4 != hi)]
    b_slot = jnp.array([0, 2, 3, 1, 4, 6, 7, 5], jnp.int32)[(numbers // 2 - y) % 4 + 4 * (numbers % 2 != lo)]
    early = (a_slot < 4) & (b_slot < 5)
    then = (a_slot < 6) & (b_slot < 7) & ~early

    def listed(mask):
        mask = mask.astype(jnp.int32)
        hit = ((jnp.cumsum(mask) - 1)[None, :] == numbers[:, None]) & (mask[None, :] == 1)
        pick = jnp.stack([a_slot, b_slot], 1)
        lists = jnp.sum(jnp.where(hit[:, :, None], pick[None], 0), 1).reshape(-1)
        return jnp.concatenate([jnp.sum(mask)[None], core[None], lists]).astype(jnp.int32)

    by_b = jnp.sum(jnp.where(b_slot[None, :] == numbers[:, None], a_slot[None, :], 0), 1)
    ids = jnp.concatenate([core[None], by_b]).astype(jnp.int32)
    list1, list2, list3 = listed(early), listed(then), listed(~early & ~then)

    zh = send(own, "zh")
    xp, xm, yp, ym = send(own, "x+"), send(own, "x-"), send(own, "y+"), send(own, "y-")
    zh, xp, xm, own_z, ids, list1, list2, list3 = lax.optimization_barrier(
        (zh, xp, xm, own, ids, list1, list2, list3)
    )
    xhp, xhm = send(zh, "x+"), send(zh, "x-")
    zl = send(own_z, "zl")
    y2 = send(yp, "y+")
    zh_c, xp_c, xm_c, own_c = send(zh, "core"), send(xp, "core"), send(xm, "core"), send(own_z, "core")
    xhp, xhm, zl, y2, xp_t = lax.optimization_barrier((xhp, xhm, zl, y2, xp))
    yzp, yzm = send(zl, "y+"), send(zl, "y-")
    x2, xh2 = send(xp_t, "x+"), send(xhm, "x-")
    pairs = [(own_z, own_c), (xp, xp_c), (xm, xm_c), (zh, zh_c)]
    b_all = [[own], [yp], [ym], [y2], [zl]]
    acc = square_part(list1, pairs, b_all, None, chunks=2)
    yzp, yzm, x2, xh2, xhp, xhm, acc = lax.optimization_barrier((yzp, yzm, x2, xh2, xhp, xhm, acc))
    half = BODY // 2
    yz2 = [send(yzp[:half], "y+"), send(yzm[half:], "y-")]
    xhp_c, xhm_c = send(xhp, "core"), send(xhm, "core")
    x2_c, xh2_c = send(x2, "core"), send(after(xh2, xhp_c), "core")
    pairs += [(xhp, xhp_c), (xhm, xhm_c)]
    b_all += [[yzp], [yzm]]
    acc = square_part(list2, pairs, b_all, acc, chunks=2)
    pairs += [(x2, x2_c), (xh2, xh2_c)]
    b_all += [yz2]
    sq, s1, s2 = square_part(list3, pairs, b_all, acc, keep=keep, chunks=2)

    notes = [own, yp, ym, y2, zl, yzp, yzm, yz2[1]]

    def add(slots, blocks, start, **kw):
        return cubic_part(ids, slots, pairs, [notes[j] for j in slots], blocks, start, **kw)

    def whole(a):
        return [(a, 0, KEEP)]

    def parted(one, *two):
        n = SECOND // len(two)
        return [(one, SECOND, FIRST)] + [(a, j * n, n) for j, a in enumerate(two)]

    cut, mid = SECOND * B, SECOND // 2 * B
    z_1 = send(s1, "zl")
    yp_s, ym_s = send(sq, "y+"), send(sq, "y-")
    acc = add([0], [whole(sq)], tiles, x_where=own_where)
    z_1, s2, acc = lax.optimization_barrier((z_1, s2, acc))
    z_2 = send(s2, "zl")
    yzp_1, yzm_1 = send(z_1, "y+"), send(z_1, "y-")
    acc = add([4], [parted(z_1, z_2)], acc)
    yp_s, ym_s, acc = lax.optimization_barrier((yp_s, ym_s, acc))
    yzp_2 = send(yp_s[:cut], "zl")
    y2_2a, y2_2b = send(yp_s[:mid], "y+"), send(ym_s[mid:cut], "y-")
    yp_1, ym_2 = yp_s[cut:], ym_s[:cut]
    acc = add([1], [whole(yp_s)], acc)
    ym_2, yzp_2, acc = lax.optimization_barrier((ym_2, yzp_2, acc))
    yzm_2 = send(ym_2, "zl")
    acc = add([2], [whole(ym_s)], acc)
    yzp_1, yzm_1, y2_2a, y2_2b, yp_1, acc = lax.optimization_barrier((yzp_1, yzm_1, y2_2a, y2_2b, yp_1, acc))
    y2_1, yz2_1 = send(yp_1, "y+"), send(yzm_1, "y-")
    acc = add([5], [parted(yzp_1, yzp_2)], acc)
    y2_2a, y2_2b, yzm_2, acc = lax.optimization_barrier((y2_2a, y2_2b, yzm_2, acc))
    yz2_2a, yz2_2b = send(y2_2a, "zl"), send(y2_2b, "zl")
    acc = add([6], [parted(yzm_1, yzm_2)], acc)
    out = add([3, 7], [parted(y2_1, y2_2a, y2_2b), parted(yz2_1, yz2_2a, yz2_2b)], acc, keep=keep)
    return out.reshape(1, 1, KEEP, B, B)


def solution(mesh):
    placed = (P("row", "col", None, None, None), P("row", "col", None), P("row", "col", None))
    return jax.shard_map(
        on_device,
        mesh=mesh,
        in_specs=placed,
        out_specs=P("row", "col", None, None, None),
        check_vma=False,
    )
```
